256 devices in a mesh: dp: 8 (over y, core), expert: 32 (over x, z).
Axes of the slice: x: 4, y: 4, z: 8, core: 2. Of those that a mesh axis runs over, the one named last changes fastest.
Arguments:
- tokens: bfloat16 [32768, 2048], P(('dp', 'expert')), may hold values from -9 to 9
- out_grad: bfloat16 [32768, 2048], P(('dp', 'expert')), may hold values from -1.8 to 1.8
- probs: bfloat16 [32768, 8], P(('dp', 'expert')), may hold values from 0.019897461 to 0.5
- expert_ids: int32 [32768, 8], P(('dp', 'expert')), may hold values from 0 to 31, all different within a row; in each aligned block of 128 rows (0 to 127, 128 to 255, ...) at most 40 rows name the same one
- dropped: int32 [32768, 8], P(('dp', 'expert')), may hold values 0 or 1
- preacts: bfloat16 [8, 32, 1280, 768], P('dp', 'expert'), may hold values from -6 to 6
- w_gu: bfloat16 [32, 2048, 768], P('expert', 'dp'), may hold values from -0.125 to 0.125
- w_down: bfloat16 [32, 384, 2048], P('expert', None, 'dp'), may hold values from -0.3125 to 0.3125
Outputs:
- tok_grad: bfloat16 [32768, 2048], P(('dp', 'expert'))
- prob_grad: bfloat16 [32768, 8], P(('dp', 'expert'))
- grad_gu: float32 [32, 2048, 768], P('expert', 'dp')
- grad_down: float32 [32, 384, 2048], P('expert', None, 'dp')
- mean_square: float32 [], replicated
The draws below stay inside these ranges and needn't reach their ends.
Inputs may be any that keep to these rules, and one draw needn't show every extreme that they name: `expert_ids`: each row names 8 different experts. Within the rows of one device no expert is named more than 40 times, a bound that some block reaches in every draw.
All inputs are finite; a program needn't handle non-finite values. No bound on the sum of `dropped` on one device may be relied on, other than what follows from the above.
Results may differ from the reference program's by a relative error of at most 0.017.
Values may be sent and summed in bfloat16 or wider, within the bound.
No kernel may reach another device: no remote copies, remote signals or barrier semaphores. Data moves between devices by JAX's collectives and lax.ppermute only.
A program may use at most 128 MiB of HBM per device.

```python
import math
import jax
import jax.numpy as jnp
import numpy as np
from jax import lax

D = 2048
TOP = 8
FW = 384
EXPERTS = 32
TOK_DEV = 128
CAP = 40
SLOTS = 1280
TOKENS = 32768
N_DP = 8
N_EXPERT = 32


def column_scale(low):
    return low + jnp.arange(D, dtype=jnp.float32) / (D - 1)


def draw_tokens(key, part):
    key = jax.random.fold_in(key, 11)
    values = jnp.clip(jax.random.normal(key, (TOKENS, D), jnp.float32), -6.0, 6.0) * column_scale(0.5)[None, :]
    return values.astype(jnp.bfloat16)


def draw_out_grad(key, part):
    key = jax.random.fold_in(key, 23)
    values = 0.3 * jnp.clip(jax.random.normal(key, (TOKENS, D), jnp.float32), -4.0, 4.0) * column_scale(0.5)[None, :]
    return values.astype(jnp.bfloat16)


def touch_ends(values, key, smallest, top_value):
    dims = values.shape
    place = [jax.random.randint(jax.random.fold_in(key, axis), (), 0, dims[axis]) for axis in range(len(dims))]
    values = values.at[tuple(place)].set(smallest)
    longest = dims.index(max(dims))
    place[longest] = (place[longest] + 1) % dims[longest]
    return values.at[tuple(place)].set(top_value)


def shard_levels(own_key, shape, pieces, smallest, largest):
    gain = 1.0
    for dim, shards_of in pieces:
        draws = jax.random.uniform(jax.random.fold_in(jax.random.fold_in(own_key, 6), dim), (shards_of,), jnp.float32, smallest / len(pieces), largest / len(pieces))
        gain = gain * jnp.repeat(jnp.exp(draws), shape[dim] // shards_of).reshape((-1,) + (1,) * (len(shape) - 1 - dim))
    return gain


def deal_out(own_key, own, number, rows, count, top, bound, slope):
    sequence = jax.random.permutation(own_key, count)
    crowded, usual = shares(count, rows * top, bound, slope, True), shares(count, rows * top, bound, slope, False)
    places = jnp.arange(count)

    def named(sizes, turn):
        used = int((sizes > 0).sum())
        fixed = max(1, used // 4)
        moved = fixed + (places - fixed + turn * (used - fixed)) % max(1, count - fixed)
        return jnp.zeros((count,), jnp.int32).at[sequence[jnp.where(places < fixed, places, moved)]].set(jnp.asarray(sizes, jnp.int32))

    sizes = jnp.where(number % 4 == 0, named(crowded, number // 4), named(usual, number - number // 4 - 1))
    mixed = jax.random.permutation(jax.random.fold_in(own, 3), count)
    giver, receiver = mixed[0:count // 2 * 2:2], mixed[1:count // 2 * 2:2]
    room = jnp.minimum(sizes[giver] - 1, bound - sizes[receiver]) // 2
    room = jnp.where((giver == sequence[0]) | (receiver == sequence[0]) | (sizes[receiver] == 0), 0, jnp.maximum(room, 0))
    moved = jax.random.randint(jax.random.fold_in(own, 4), (count // 2,), 0, 1 << 20) % (room + 1)
    sizes = sizes.at[giver].add(-moved).at[receiver].add(moved)
    items = jnp.searchsorted(jnp.cumsum(sizes), jnp.arange(rows * top), side="right").astype(jnp.int32)
    grid = items.reshape(top, rows).T
    grid = grid[jax.random.permutation(jax.random.fold_in(own, 1), rows)]
    turn = jax.random.randint(jax.random.fold_in(own, 2), (rows, 1), 0, top)
    return jnp.take_along_axis(grid, (jnp.arange(top)[None, :] + turn) % top, axis=1)


def shares(count, total, reach, lean, full):
    loads = [(1 << 20) // math.isqrt(rank ** lean) + 1 for rank in range(1, count + 1)]
    largest = reach if full else min(reach, max(-(-total // count), total * loads[0] // sum(loads)))
    least = 1 if total - largest >= count - 1 else 0
    holding, spare = [largest] + [least] * (count - 1), total - largest - least * (count - 1)
    while spare > 0:
        free = [i for i in range(1, count) if holding[i] < largest] or [i for i in range(1, count) if holding[i] < reach]
        mass, budget = sum([loads[i] for i in free]), spare
        for i in free:
            addition = min(reach - holding[i], max(1, budget * loads[i] // mass), spare)
            holding[i] = holding[i] + addition
            spare = spare - addition
    return np.array(holding)


def centred(key, shape, scale, limit, shards=(), kind=jnp.bfloat16):
    values = scale * jax.random.normal(key, shape, jnp.float32)
    if shards:
        values = values * shard_levels(key, shape, shards, -0.22, 0.18)
    return jnp.clip(values, -limit, limit).astype(kind)


def setup_inputs(seed: int = 0) -> dict:
    splits = jax.random.split(jax.random.key(seed), 9)
    tokens = draw_tokens(jax.random.fold_in(splits[8], 71), 0)
    out_grad = draw_out_grad(jax.random.fold_in(splits[8], 71), 0)
    probs = jnp.clip(jnp.exp(math.log(0.5) - 3.224016 * jax.random.uniform(splits[2], (TOKENS, TOP), jnp.float32) ** shard_levels(splits[2], (TOKENS, TOP), ((0, 256),), -0.2, 0.2)), 0.019897461, 0.5).astype(jnp.bfloat16)
    expert_ids_keys = jax.random.split(jax.random.fold_in(splits[3], 1), TOKENS // TOK_DEV)
    expert_ids_turns = jax.random.permutation(jax.random.fold_in(splits[3], 3), TOKENS // TOK_DEV)
    expert_ids = jax.vmap(lambda own, number: deal_out(jax.random.fold_in(splits[3], 2), own, number, TOK_DEV, EXPERTS, TOP, CAP, 2))(expert_ids_keys, expert_ids_turns).reshape((TOKENS, TOP))
    dropped = touch_ends((jax.random.randint(splits[4], (TOKENS, TOP), 0, 8) < 1).astype(jnp.int32), jax.random.fold_in(splits[4], 1), 0, 1)
    preacts = centred(splits[5], (N_DP, EXPERTS, SLOTS, 2 * FW), 1.0, 6.0, ((0, 8), (1, 32)))
    w_gu = centred(splits[6], (EXPERTS, D, 2 * FW), D ** -0.5, 0.125, ((0, 32), (1, 8)))
    w_down = centred(splits[7], (EXPERTS, FW, D), FW ** -0.5, 0.3125, ((0, 32), (2, 8)))
    return dict(tokens=tokens, out_grad=out_grad, probs=probs, expert_ids=expert_ids, dropped=dropped, preacts=preacts, w_gu=w_gu, w_down=w_down)


def slot_match(expert_ids, dropped, experts, capacity):
    tok_rows, top_k = expert_ids.shape
    flat_ids = expert_ids.reshape(-1)
    onehot = (flat_ids[:, None] == jnp.arange(experts, dtype=jnp.int32)[None, :]).astype(jnp.int32)
    before = jnp.cumsum(onehot, axis=0) - onehot
    position = jnp.sum(before * onehot, axis=1).astype(jnp.int32)
    slot_ids = flat_ids * capacity + position
    slot_ids = jnp.where(dropped.reshape(-1) == 0, slot_ids, -1).reshape(tok_rows, top_k)
    every_slot = jnp.arange(experts * capacity, dtype=jnp.int32)
    return (every_slot[:, None, None] == slot_ids[None, :, :]).astype(jnp.float32)


def reference(tokens, out_grad, probs, expert_ids, dropped, preacts, w_gu, w_down):
    w_gu_f = w_gu.astype(jnp.float32)
    w_down_f = w_down.astype(jnp.float32)

    def row_pass(carry, row_data):
        tokens_row, grad_row, probs_row, ids_row, drop_row, pre_row = row_data
        matches = jax.vmap(slot_match, in_axes=(0, 0, None, None))(ids_row, drop_row, EXPERTS, CAP)
        counts = jnp.sum(matches, axis=3)
        x_in = jnp.einsum('jqt,jtd->jqd', counts, tokens_row.astype(jnp.float32)).astype(jnp.bfloat16)
        grad_in = jnp.einsum('jqt,jtd->jqd', counts, grad_row.astype(jnp.float32)).astype(jnp.bfloat16)
        x_in = x_in.reshape(N_EXPERT, EXPERTS, CAP, D)
        grad_in = grad_in.reshape(N_EXPERT, EXPERTS, CAP, D)
        prob_in = jnp.einsum('jqtk,jtk->jq', matches, probs_row.astype(jnp.float32)).astype(jnp.bfloat16)
        prob_in = prob_in.reshape(N_EXPERT, EXPERTS, CAP)
        pre_acts = pre_row.reshape(EXPERTS, N_EXPERT, CAP, 2 * FW).astype(jnp.float32)
        proj = jnp.einsum('jecd,efd->ejcf', grad_in.astype(jnp.float32), w_down_f)
        gate_pre = pre_acts[..., :FW]
        up_pre = pre_acts[..., FW:]
        sigmoid_a = jax.nn.sigmoid(gate_pre)
        silu_a = gate_pre * sigmoid_a
        hidden = silu_a * up_pre
        slot_prob = jnp.sum(hidden * proj, axis=-1).astype(jnp.bfloat16)
        weight_p = jnp.transpose(prob_in, (1, 0, 2)).astype(jnp.float32)[..., None]
        scaled = weight_p * proj
        dgu = jnp.concatenate([scaled * up_pre * sigmoid_a * (1.0 + gate_pre * (1.0 - sigmoid_a)), scaled * silu_a], axis=-1).astype(jnp.bfloat16)
        slot_grad = jnp.einsum('ejcf,edf->jecd', dgu.astype(jnp.float32), w_gu_f).astype(jnp.bfloat16)
        hidden_p = (weight_p * hidden).astype(jnp.bfloat16)
        grad_gu_row = jnp.einsum('jecd,ejcf->edf', x_in.astype(jnp.float32), dgu.astype(jnp.float32))
        grad_down_row = jnp.einsum('ejcf,jecd->efd', hidden_p.astype(jnp.float32), grad_in.astype(jnp.float32))
        slot_flat = slot_grad.reshape(N_EXPERT, EXPERTS * CAP, D).astype(jnp.float32)
        tok_grad_row = jnp.einsum('jqt,jqd->jtd', counts, slot_flat).astype(jnp.bfloat16)
        prob_slot = jnp.transpose(slot_prob, (1, 0, 2)).reshape(N_EXPERT, EXPERTS * CAP).astype(jnp.float32)
        prob_grad_row = jnp.einsum('jqtk,jq->jtk', matches, prob_slot).astype(jnp.bfloat16)
        return (carry[0] + grad_gu_row, carry[1] + grad_down_row), (tok_grad_row, prob_grad_row)

    start = (jnp.zeros((EXPERTS, D, 2 * FW), jnp.float32), jnp.zeros((EXPERTS, FW, D), jnp.float32))
    row_inputs = (tokens.reshape(N_DP, N_EXPERT, TOK_DEV, D), out_grad.reshape(N_DP, N_EXPERT, TOK_DEV, D),
                  probs.reshape(N_DP, N_EXPERT, TOK_DEV, TOP), expert_ids.reshape(N_DP, N_EXPERT, TOK_DEV, TOP),
                  dropped.reshape(N_DP, N_EXPERT, TOK_DEV, TOP), preacts)
    (grad_gu, grad_down), (tok_grad, prob_grad) = lax.scan(row_pass, start, row_inputs)
    total = jnp.sum(grad_gu * grad_gu) + jnp.sum(grad_down * grad_down)
    mean_square = total / (EXPERTS * 3 * D * FW)
    return (tok_grad.reshape(TOKENS, D), prob_grad.reshape(TOKENS, TOP), grad_gu, grad_down, mean_square)
```

```python
import jax
import jax.numpy as jnp
from jax import lax
from jax.sharding import Mesh, PartitionSpec as P

D = 2048
FW = 384
EXPERTS = 32
CAP = 40
TOK = 128
NX = 4
NZ = 8
CHUNKS = 2
WIDTH = D // CHUNKS
BF = jnp.bfloat16
F32 = jnp.float32


def shift(a, step):
    return lax.ppermute(a, "z", [(i, (i + step) % NZ) for i in range(NZ)])


def gather_z(block):
    half = block.shape[1] // 2
    forth, back = block, block
    blocks = [block] + [None] * 7
    for step in (1, 2, 3):
        forth, back = shift(forth, 1), shift(back, -1)
        blocks[NZ - step], blocks[step] = forth, back
    blocks[4] = jnp.concatenate([shift(forth[:, :half], 1), shift(back[:, half:], -1)], axis=1)
    return jnp.stack(blocks)


def add_to(part, got):
    return (part.astype(F32) + got.astype(F32)).astype(BF)


def reduce_z(parts):
    half = parts.shape[2] // 2
    forth, back = shift(parts[4][:, :half], 1), shift(parts[4][:, half:], -1)
    forth = jnp.concatenate([add_to(parts[3][:, :half], forth), parts[3][:, half:]], axis=1)
    back = jnp.concatenate([parts[5][:, :half], add_to(parts[5][:, half:], back)], axis=1)
    for ahead, behind in ((2, 6), (1, 7)):
        forth = add_to(parts[ahead], shift(forth, 1))
        back = add_to(parts[behind], shift(back, -1))
    forth, back = shift(forth, 1), shift(back, -1)
    return (parts[0].astype(F32) + forth.astype(F32) + back.astype(F32)).astype(BF)


def exchange_x(a):
    return lax.all_to_all(a, "x", split_axis=0, concat_axis=0, tiled=True)


def turned(a, axis, start):
    return lax.dynamic_slice_in_dim(jnp.concatenate([a, a], axis=axis), start, NZ, axis)


def slot_map(ids, dropped, probs):
    experts = jnp.arange(EXPERTS, dtype=jnp.int32)
    named = ids.T[None, :, :] == experts[:, None, None]
    routed = jnp.any(named, axis=1)
    kept = jnp.any(named & (dropped.T == 0)[None], axis=1)
    order = jnp.arange(TOK, dtype=jnp.int32)
    earlier = (order[:, None] < order[None, :]).astype(BF)
    position = jnp.dot(routed.astype(BF), earlier, preferred_element_type=F32)
    slots = jnp.where(kept, position, -1.0)
    weights = jnp.sum(jnp.where(named, probs.T.astype(F32)[None], 0.0), axis=1)
    return slots.astype(BF), weights.astype(BF)


def body(tokens, out_grad, probs, expert_ids, dropped, preacts, w_gu, w_down):
    x, z = lax.axis_index("x"), lax.axis_index("z")
    slots, weights = slot_map(expert_ids, dropped, probs)
    info = lax.all_gather(jnp.stack([slots, weights]), ("x", "z"), axis=0, tiled=False)
    w_down_full = lax.all_gather(w_down, ("y", "c"), axis=2, tiled=True)[0]
    w_gu_full = lax.all_gather(w_gu, ("y", "c"), axis=1, tiled=True)[0]
    places = jnp.arange(CAP, dtype=jnp.int32).astype(F32)

    info = info.reshape(NX, NZ, 2, NX, NZ, TOK)
    mine = turned(lax.dynamic_index_in_dim(info[:, :, 0], x, 0, keepdims=False), 0, z)
    mine = lax.dynamic_index_in_dim(mine, z, 2, keepdims=False).astype(F32)
    onehot = (mine[:, :, None, :] == places[None, None, :, None]).astype(BF)
    onehot = onehot.reshape(NZ, NX * CAP, TOK)

    own = lax.dynamic_index_in_dim(lax.dynamic_index_in_dim(info, x, 3, keepdims=False), z, 3, keepdims=False)
    own = turned(own, 1, z).astype(F32)
    held = own[:, :, 0, None, :] == places[None, None, :, None]
    prob_in = jnp.sum(jnp.where(held, own[:, :, 1, None, :], 0.0), axis=-1).reshape(-1)

    pre = turned(preacts.reshape(NX, NZ, CAP, 2 * FW), 1, z).reshape(NX * NZ * CAP, 2 * FW)

    def to_slots(piece):
        blocks = gather_z(piece)
        rows = jnp.einsum("ost,otd->osd", onehot, blocks, preferred_element_type=F32).astype(BF)
        rows = rows.reshape(NZ, NX, CAP, WIDTH).transpose(1, 0, 2, 3)
        return exchange_x(rows.reshape(NX, NZ * CAP, WIDTH)).reshape(NX * NZ * CAP, WIDTH)

    cuts = [slice(i * WIDTH, (i + 1) * WIDTH) for i in range(CHUNKS)]
    grad_in = [to_slots(out_grad[:, cut]) for cut in cuts]
    x_in = [to_slots(tokens[:, cut]) for cut in cuts]

    proj = 0.0
    for cut, piece in zip(cuts, grad_in):
        proj = proj + jnp.einsum("qd,fd->qf", piece, w_down_full[:, cut], preferred_element_type=F32)
    gate_pre = pre[:, :FW].astype(F32)
    up_pre = pre[:, FW:].astype(F32)
    sigmoid_a = jax.nn.sigmoid(gate_pre)
    silu_a = gate_pre * sigmoid_a
    hidden = silu_a * up_pre
    slot_prob = jnp.sum(hidden * proj, axis=-1).astype(BF)
    scaled = prob_in[:, None] * proj
    dgu = jnp.concatenate(
        [scaled * up_pre * sigmoid_a * (1.0 + gate_pre * (1.0 - sigmoid_a)), scaled * silu_a], axis=-1
    ).astype(BF)
    hidden_p = (prob_in[:, None] * hidden).astype(BF)

    tok_grad = []
    for cut in cuts:
        slot_grad = jnp.einsum("qf,df->qd", dgu, w_gu_full[cut], preferred_element_type=F32).astype(BF)
        back = exchange_x(slot_grad.reshape(NX, NZ * CAP, WIDTH))
        back = back.reshape(NX, NZ, CAP, WIDTH).transpose(1, 0, 2, 3).reshape(NZ, NX * CAP, WIDTH)
        parts = jnp.einsum("ost,osd->otd", onehot, back, preferred_element_type=F32).astype(BF)
        tok_grad.append(reduce_z(parts))
    tok_grad = jnp.concatenate(tok_grad, axis=1)

    grad_down = jnp.concatenate(
        [jnp.einsum("qf,qd->fd", hidden_p, p, preferred_element_type=F32) for p in grad_in], axis=1
    ).astype(BF)
    grad_gu = jnp.concatenate(
        [jnp.einsum("qd,qf->df", p, dgu, preferred_element_type=F32) for p in x_in], axis=0
    ).astype(BF)
    grad_down = lax.psum_scatter(grad_down[None], ("y", "c"), scatter_dimension=2, tiled=True).astype(F32)
    grad_gu = lax.psum_scatter(grad_gu[None], ("y", "c"), scatter_dimension=1, tiled=True).astype(F32)

    straight = turned(slot_prob.reshape(NX, NZ, CAP), 1, (NZ - z) % NZ)
    prob_all = lax.all_gather(straight, ("x", "z"), axis=0, tiled=False)
    prob_all = lax.dynamic_index_in_dim(prob_all, x, 1, keepdims=False)
    prob_all = lax.dynamic_index_in_dim(prob_all, z, 1, keepdims=False).astype(F32)
    hit = slots.astype(F32)[:, None, :] == places[None, :, None]
    by_expert = jnp.sum(jnp.where(hit, prob_all[:, :, None], 0.0), axis=1)
    experts = jnp.arange(EXPERTS, dtype=jnp.int32)
    named = expert_ids.T[:, None, :] == experts[None, :, None]
    prob_grad = jnp.sum(jnp.where(named, by_expert[None], 0.0), axis=1).T.astype(BF)

    partial_sq = jnp.sum(grad_gu * grad_gu) + jnp.sum(grad_down * grad_down)
    total = lax.psum(partial_sq, ("y", "c", "x", "z"))
    mean_square = total / (EXPERTS * 3 * D * FW)
    return tok_grad, prob_grad, grad_gu, grad_down, mean_square


def solution(mesh):
    split = Mesh(mesh.devices.reshape(4, 2, NX, NZ), ("y", "c", "x", "z"))
    rows = P(("y", "c", "x", "z"), None)
    gu, down = P(("x", "z"), ("y", "c"), None), P(("x", "z"), None, ("y", "c"))
    return jax.shard_map(
        body,
        mesh=split,
        in_specs=(rows, rows, rows, rows, rows, P(("y", "c"), ("x", "z"), None, None), gu, down),
        out_specs=(rows, rows, gu, down, P()),
        check_vma=False,
    )
```

```python
import jax
import jax.numpy as jnp
from jax import lax
from jax.sharding import Mesh, PartitionSpec as P

D = 2048
FW = 384
EXPERTS = 32
CAP = 40
TOK = 128
NX = 4
NZ = 8
CHUNKS = 2
WIDTH = D // CHUNKS
BF = jnp.bfloat16
F32 = jnp.float32


def shift(a, step):
    return lax.ppermute(a, "z", [(i, (i + step) % NZ) for i in range(NZ)])


def gather_z(block):
    half = block.shape[1] // 256 * 128
    forth, back = block, block
    blocks = [block] + [None] * 7
    for step in (1, 2, 3):
        forth, back = shift(forth, 1), shift(back, -1)
        blocks[NZ - step], blocks[step] = forth, back
    blocks[4] = jnp.concatenate([shift(forth[:, :half], 1), shift(back[:, half:], -1)], axis=1)
    return jnp.stack(blocks), blocks[2]


def add_to(part, got):
    return (part.astype(F32) + got.astype(F32)).astype(BF)


def reduce_z(parts):
    half = parts.shape[2] // 256 * 128
    forth, back = shift(parts[4][:, :half], 1), shift(parts[4][:, half:], -1)
    forth = jnp.concatenate([add_to(parts[3][:, :half], forth), parts[3][:, half:]], axis=1)
    back = jnp.concatenate([parts[5][:, :half], add_to(parts[5][:, half:], back)], axis=1)
    for ahead, behind in ((2, 6), (1, 7)):
        forth = add_to(parts[ahead], shift(forth, 1))
        back = add_to(parts[behind], shift(back, -1))
    forth, back = shift(forth, 1), shift(back, -1)
    return (parts[0].astype(F32) + forth.astype(F32) + back.astype(F32)).astype(BF)


def exchange_x(a):
    return lax.all_to_all(a, "x", split_axis=0, concat_axis=0, tiled=True)


def turned(a, axis, start):
    return lax.dynamic_slice_in_dim(jnp.concatenate([a, a], axis=axis), start, NZ, axis)


def slot_map(ids, dropped, probs):
    experts = jnp.arange(EXPERTS, dtype=jnp.int32)
    named = ids.T[:, :, None] == experts[None, None, :]
    routed = jnp.any(named, axis=0)
    kept = jnp.any(named & (dropped.T == 0)[:, :, None], axis=0)
    order = jnp.arange(TOK, dtype=jnp.int32)
    earlier = (order[:, None] > order[None, :]).astype(BF)
    position = jnp.dot(earlier, routed.astype(BF), preferred_element_type=F32)
    slots = jnp.where(kept, position, -1.0)
    weights = jnp.sum(jnp.where(named, probs.T.astype(F32)[:, :, None], 0.0), axis=0)
    return slots.astype(BF), weights.astype(BF)


def total_of(value):
    value = jnp.full((8, 128), value, F32)
    for axis, size, width in (("c", 2, 2), ("y", 4, 4), ("x", 4, 4), ("z", 8, 4), ("z", 8, 8)):
        unit = 4 if width == 8 else 1
        others = [
            lax.ppermute(value, axis, [(i, i ^ (unit * k)) for i in range(size)])
            for k in range(1, width // unit)
        ]
        if len(others) == 1:
            value = value + others[0]
        else:
            value = (value + others[0]) + (others[1] + others[2])
    return value[0, 0]


def after(value, earlier):
    return lax.optimization_barrier((value, earlier))[0]


def body(tokens, out_grad, probs, expert_ids, dropped, preacts, w_gu, w_down):
    x, z = lax.axis_index("x"), lax.axis_index("z")
    slots, weights = slot_map(expert_ids, dropped, probs)
    w_down_full = lax.all_gather(w_down, ("y", "c"), axis=2, tiled=True)[0]
    w_gu_full = lax.all_gather(w_gu, ("y", "c"), axis=1, tiled=True)[0]
    places = jnp.arange(CAP, dtype=jnp.int32).astype(F32)
    lane = jnp.arange(128, dtype=jnp.int32)[None, :]
    info = jnp.concatenate([slots, weights, jnp.zeros((TOK, 64), BF)], axis=1)
    pre = turned(preacts.reshape(NX, NZ, CAP, 2 * FW), 1, z).reshape(NX * NZ * CAP, 2 * FW)
    cuts = [slice(i * WIDTH, (i + 1) * WIDTH) for i in range(CHUNKS)]

    pieces = [out_grad[:, cut] for cut in cuts] + [tokens[:, cut] for cut in cuts]
    pieces[0] = jnp.concatenate([pieces[0], info], axis=1)
    gathered, mark = [], None
    for piece in pieces:
        blocks, mark = gather_z(piece if mark is None else after(piece, mark))
        gathered.append(blocks)
    maps = gathered[0][:, :, WIDTH : WIDTH + EXPERTS].reshape(NZ, TOK, NX, NZ)
    maps = lax.dynamic_index_in_dim(maps, z, 3, keepdims=False).transpose(0, 2, 1).astype(F32)
    onehot = (maps[:, :, None, :] == places[None, None, :, None]).astype(BF)
    onehot = onehot.reshape(NZ, NX * CAP, TOK)

    def to_slots(blocks):
        width = blocks.shape[2]
        rows = jnp.einsum("ost,otd->osd", onehot, blocks, preferred_element_type=F32).astype(BF)
        rows = rows.reshape(NZ, NX, CAP, width).transpose(1, 0, 2, 3)
        return exchange_x(rows.reshape(NX, NZ * CAP, width)).reshape(NX * NZ * CAP, width)

    received = [to_slots(blocks) for blocks in gathered]
    grad_in = [received[0][:, :WIDTH]] + received[1:CHUNKS]
    x_in = received[CHUNKS:]
    tag = received[0][:, WIDTH:].astype(F32)
    prob_in = jnp.sum(jnp.where(lane == EXPERTS + x * NZ + z, tag, 0.0), axis=1)

    proj = 0.0
    for cut, piece in zip(cuts, grad_in):
        proj = proj + jnp.einsum("qd,fd->qf", piece, w_down_full[:, cut], preferred_element_type=F32)
    gate_pre = pre[:, :FW].astype(F32)
    up_pre = pre[:, FW:].astype(F32)
    sigmoid_a = jax.nn.sigmoid(gate_pre)
    silu_a = gate_pre * sigmoid_a
    hidden = silu_a * up_pre
    slot_prob = jnp.sum(hidden * proj, axis=-1).astype(BF)
    scaled = prob_in[:, None] * proj
    dgu = jnp.concatenate(
        [scaled * up_pre * sigmoid_a * (1.0 + gate_pre * (1.0 - sigmoid_a)), scaled * silu_a], axis=-1
    ).astype(BF)
    hidden_p = (prob_in[:, None] * hidden).astype(BF)

    returned = []
    for number, cut in enumerate(cuts):
        slot_grad = jnp.einsum("qf,df->qd", dgu, w_gu_full[cut], preferred_element_type=F32).astype(BF)
        if number == 0:
            tag = jnp.where(lane == x * NZ + z, slot_prob[:, None], jnp.zeros((), BF))
            slot_grad = jnp.concatenate([slot_grad, tag], axis=1)
        width = slot_grad.shape[1]
        back = exchange_x(slot_grad.reshape(NX, NZ * CAP, width))
        back = back.reshape(NX, NZ, CAP, width).transpose(1, 0, 2, 3).reshape(NZ, NX * CAP, width)
        parts = jnp.einsum("ost,osd->otd", onehot, back, preferred_element_type=F32).astype(BF)
        returned.append(reduce_z(parts))
    tok_grad = jnp.concatenate([returned[0][:, :WIDTH]] + returned[1:], axis=1)
    by_expert = returned[0][:, WIDTH : WIDTH + EXPERTS].astype(F32).T
    experts = jnp.arange(EXPERTS, dtype=jnp.int32)
    named = expert_ids.T[:, None, :] == experts[None, :, None]
    prob_grad = jnp.sum(jnp.where(named, by_expert[None], 0.0), axis=1)
    prob_grad = jnp.where(dropped.T == 0, prob_grad, 0.0).T.astype(BF)

    grad_down = jnp.concatenate(
        [jnp.einsum("qf,qd->fd", hidden_p, p, preferred_element_type=F32) for p in grad_in], axis=1
    ).astype(BF)
    grad_gu = jnp.concatenate(
        [jnp.einsum("qd,qf->df", p, dgu, preferred_element_type=F32) for p in x_in], axis=0
    ).astype(BF)
    grad_down = lax.psum_scatter(grad_down[None], ("y", "c"), scatter_dimension=2, tiled=True).astype(F32)
    grad_gu = lax.psum_scatter(grad_gu[None], ("y", "c"), scatter_dimension=1, tiled=True).astype(F32)
    partial_sq = jnp.sum(grad_gu * grad_gu) + jnp.sum(grad_down * grad_down)
    mean_square = total_of(partial_sq) / (EXPERTS * 3 * D * FW)
    return tok_grad, prob_grad, grad_gu, grad_down, mean_square


def solution(mesh):
    split = Mesh(mesh.devices.reshape(4, 2, NX, NZ), ("y", "c", "x", "z"))
    rows = P(("y", "c", "x", "z"), None)
    gu, down = P(("x", "z"), ("y", "c"), None), P(("x", "z"), None, ("y", "c"))
    return jax.shard_map(
        body,
        mesh=split,
        in_specs=(rows, rows, rows, rows, rows, P(("y", "c"), ("x", "z"), None, None), gu, down),
        out_specs=(rows, rows, gu, down, P()),
        check_vma=False,
    )
```

```python
import functools
import jax
import jax.numpy as jnp
from jax import lax
from jax.experimental import pallas as pl
from jax.experimental.pallas import tpu as pltpu
from jax.sharding import Mesh, PartitionSpec as P

D = 2048
FW = 384
EXPERTS = 32
CAP = 40
TOK = 128
NX = 4
NZ = 8
WIDTH = 1024
BACK = 1024
BF = jnp.bfloat16
F32 = jnp.float32


def shift(a, step):
    return lax.ppermute(a, "z", [(i, (i + step) % NZ) for i in range(NZ)])


def gather_z(block):
    half = block.shape[1] // 256 * 128
    forth, back = block, block
    blocks = [block] + [None] * 7
    for step in (1, 2, 3):
        forth, back = shift(forth, 1), shift(back, -1)
        blocks[NZ - step], blocks[step] = forth, back
    blocks[4] = shift(forth[:, :half], 1)
    blocks.append(shift(back[:, half:], -1))
    return blocks


def slot_rows(which, block, out_ref, pair, span):
    places = lax.broadcasted_iota(jnp.int32, (CAP, TOK), 0).astype(F32)
    halves = []
    for number in range(2):
        hits = [jnp.where(which(2 * pair + number, e) == places, 1.0, 0.0) for e in range(NX)]
        hits = jnp.concatenate(hits, axis=0).astype(BF)
        halves.append(jnp.dot(hits, block(2 * pair + number), preferred_element_type=F32))
    for e in range(NX):
        rows = [half[e * CAP : (e + 1) * CAP] for half in halves]
        out_ref[e, pl.ds(pair * 2 * CAP, 2 * CAP), span] = jnp.concatenate(rows, axis=0).astype(BF)


def spans(width):
    return [slice(at, min(at + 384, width)) for at in range(0, width, 384)]


def place_blocks(z, refs, held):
    width = held.shape[2]
    half = refs[4].shape[1]
    for ahead in range(NZ):
        at = lax.rem(z + ahead, NZ)
        if ahead == 4:
            held[at, :, :half] = refs[4][...]
            held[at, :, half:] = refs[8][...]
        else:
            held[at] = refs[ahead][...]


def first_kernel(z_ref, *refs):
    blocks, (out_ref, map_ref, held, flipped) = refs[:9], refs[10:]
    z = z_ref[0]
    place_blocks(z, blocks, held)
    for at in range(NZ):
        flipped[...] = held[at, :, WIDTH:].astype(F32).T
        for e in range(NX):
            map_ref[at, e : e + 1, :] = flipped[pl.ds(e * NZ + z, 1), :]
        map_ref[at, NX:, :] = jnp.zeros((8 - NX, TOK), F32)
    for span in spans(held.shape[2]):
        for pair in range(NZ // 2):
            slot_rows(lambda k, e: map_ref[k, e : e + 1, :], lambda k: held[k, :, span], out_ref, pair, span)


def later_kernel(z_ref, map_ref, *refs):
    blocks, (out_ref, held) = refs[:9], refs[10:]
    place_blocks(z_ref[0], blocks, held)
    for span in spans(held.shape[2]):
        for pair in range(NZ // 2):
            slot_rows(lambda k, e: map_ref[k, e : e + 1, :], lambda k: held[k, :, span], out_ref, pair, span)


def whole_kernel(map_ref, rows_ref, out_ref):
    for pair in range(NZ // 2):
        slot_rows(
            lambda k, e: map_ref[k, e : e + 1, :],
            lambda k: rows_ref[k * TOK : (k + 1) * TOK, :],
            out_ref,
            pair,
            slice(None),
        )


VMEM = pl.BlockSpec(memory_space=pltpu.VMEM)
SMEM = pl.BlockSpec(memory_space=pltpu.SMEM)
PARAMS = pltpu.CompilerParams(vmem_limit_bytes=56 * 1024 * 1024)


def cost_of(width):
    return pl.CostEstimate(
        flops=2 * NZ * NX * CAP * TOK * width, bytes_accessed=2 * (NZ * TOK + NX * NZ * CAP) * width, transcendentals=0
    )


def slots_first(z, blocks, earlier):
    width = blocks[0].shape[1]
    return pl.pallas_call(
        first_kernel,
        out_shape=(
            jax.ShapeDtypeStruct((NX, NZ * CAP, width), BF),
            jax.ShapeDtypeStruct((NZ, 8, TOK), F32),
        ),
        in_specs=[SMEM] + [VMEM] * 9 + [pl.BlockSpec(memory_space=pl.ANY)],
        out_specs=(VMEM, VMEM),
        scratch_shapes=[pltpu.VMEM((NZ, TOK, width), BF), pltpu.VMEM((128, TOK), F32)],
        compiler_params=PARAMS,
        cost_estimate=cost_of(width),
    )(z.reshape(1), *blocks, earlier)


def slots_later(z, maps, blocks, earlier):
    width = blocks[0].shape[1]
    return pl.pallas_call(
        later_kernel,
        out_shape=jax.ShapeDtypeStruct((NX, NZ * CAP, width), BF),
        in_specs=[SMEM] + [VMEM] * 10 + [pl.BlockSpec(memory_space=pl.ANY)],
        out_specs=VMEM,
        scratch_shapes=[pltpu.VMEM((NZ, TOK, width), BF)],
        compiler_params=PARAMS,
        cost_estimate=cost_of(width),
    )(z.reshape(1), maps, *blocks, earlier)


def slots_whole(maps, rows, part, width):
    tile = 512
    return pl.pallas_call(
        whole_kernel,
        out_shape=jax.ShapeDtypeStruct((NX, NZ * CAP, width), BF),
        grid=(width // tile,),
        in_specs=[
            pl.BlockSpec((NZ, 8, TOK), lambda j: (0, 0, 0)),
            pl.BlockSpec((NZ * TOK, tile), lambda j: (0, part * (width // tile) + j)),
        ],
        out_specs=pl.BlockSpec((NX, NZ * CAP, tile), lambda j: (0, 0, j)),
        compiler_params=PARAMS,
        cost_estimate=cost_of(width),
    )(maps, rows)


def expert_kernel(e_ref, first_ref, second_ref, down_ref, pre_ref, dgu_ref, hidden_ref, tag_ref):
    expert = e_ref[0]
    sides = (((1,), (1,)), ((), ()))
    proj = lax.dot_general(first_ref[:, :WIDTH], down_ref[:, :WIDTH], sides, preferred_element_type=F32)
    proj += lax.dot_general(second_ref[...], down_ref[:, WIDTH:], sides, preferred_element_type=F32)
    lane = lax.broadcasted_iota(jnp.int32, (proj.shape[0], 128), 1)
    tag = first_ref[:, WIDTH:].astype(F32)
    prob = jnp.sum(jnp.where(lane == EXPERTS + expert, tag, 0.0), axis=1, keepdims=True)
    gate = pre_ref[:, :FW].astype(F32)
    up = pre_ref[:, FW:].astype(F32)
    sigmoid = jax.nn.sigmoid(gate)
    silu = gate * sigmoid
    hidden = silu * up
    slot_prob = jnp.sum(hidden * proj, axis=1, keepdims=True)
    scaled = prob * proj
    dgu_ref[:, :FW] = (scaled * up * sigmoid * (1.0 + gate * (1.0 - sigmoid))).astype(BF)
    dgu_ref[:, FW:] = (scaled * silu).astype(BF)
    hidden_ref[...] = (prob * hidden).astype(BF)
    tag_ref[...] = jnp.where(lane == expert, slot_prob, 0.0).astype(BF)


def expert_pass(expert, first, second, down, pre):
    rows = NZ * CAP
    slots = NX * rows
    row_block = lambda width: pl.BlockSpec((rows, width), lambda j: (j, 0))
    return pl.pallas_call(
        expert_kernel,
        out_shape=(
            jax.ShapeDtypeStruct((slots, 2 * FW), BF),
            jax.ShapeDtypeStruct((slots, FW), BF),
            jax.ShapeDtypeStruct((slots, 128), BF),
        ),
        grid=(NX,),
        in_specs=[
            SMEM,
            row_block(WIDTH + 128),
            row_block(WIDTH),
            pl.BlockSpec((FW, D), lambda j: (0, 0)),
            row_block(2 * FW),
        ],
        out_specs=(row_block(2 * FW), row_block(FW), row_block(128)),
        compiler_params=PARAMS,
        cost_estimate=pl.CostEstimate(flops=2 * slots * FW * D, bytes_accessed=12_000_000, transcendentals=slots * FW),
    )(expert.reshape(1), first, second, down, pre)


def slot_grad_kernel(start, stop, tagged, dgu_ref, up_ref, tag_ref, earlier_ref, out_ref):
    width = stop - start
    sides = (((1,), (1,)), ((), ()))
    out_ref[0, :, :width] = lax.dot_general(
        dgu_ref[...], up_ref[start:stop, :], sides, preferred_element_type=F32
    ).astype(BF)
    if tagged:
        out_ref[0, :, width:] = tag_ref[...]


def slot_grads(dgu, up, tag, earlier, start, stop, tagged):
    rows = NZ * CAP
    width = stop - start + (128 if tagged else 0)
    return pl.pallas_call(
        functools.partial(slot_grad_kernel, start, stop, tagged),
        out_shape=jax.ShapeDtypeStruct((NX, rows, width), BF),
        grid=(NX,),
        in_specs=[
            pl.BlockSpec((rows, 2 * FW), lambda j: (j, 0)),
            pl.BlockSpec((D, 2 * FW), lambda j: (0, 0)),
            pl.BlockSpec((rows, 128), lambda j: (j, 0)),
            pl.BlockSpec(memory_space=pl.ANY),
        ],
        out_specs=pl.BlockSpec((1, rows, width), lambda j: (j, 0, 0)),
        compiler_params=PARAMS,
        cost_estimate=pl.CostEstimate(
            flops=2 * NX * rows * 2 * FW * width, bytes_accessed=8_000_000, transcendentals=0
        ),
    )(dgu, up, tag, earlier)


def combine_kernel(map_ref, rows_ref, *refs):
    out_ref = refs[-1]
    places = lax.broadcasted_iota(jnp.int32, (CAP, TOK), 0).astype(F32)
    nothing = jnp.zeros((CAP, TOK), F32)
    width = rows_ref.shape[2]
    for pair in range(NZ // 2):
        hits = []
        for e in range(NX):
            here = [jnp.where(map_ref[2 * pair + n, e : e + 1, :] == places, 1.0, 0.0) for n in range(2)]
            hits.append(jnp.concatenate([here[0], nothing], axis=1))
            hits.append(jnp.concatenate([nothing, here[1]], axis=1))
        hits = jnp.concatenate(hits, axis=0).astype(BF)
        for span in spans(width):
            rows = [rows_ref[e, pair * 2 * CAP : (pair + 1) * 2 * CAP, span] for e in range(NX)]
            rows = jnp.concatenate(rows, axis=0)
            got = lax.dot_general(hits, rows, (((0,), (0,)), ((), ())), preferred_element_type=F32).astype(BF)
            out_ref[2 * pair, :, span] = got[:TOK]
            out_ref[2 * pair + 1, :, span] = got[TOK:]


def combine(maps, rows, *earlier):
    width = rows.shape[2]
    return pl.pallas_call(
        combine_kernel,
        out_shape=jax.ShapeDtypeStruct((NZ, TOK, width), BF),
        in_specs=[VMEM, VMEM] + [pl.BlockSpec(memory_space=pl.ANY)] * len(earlier),
        out_specs=VMEM,
        compiler_params=PARAMS,
        cost_estimate=cost_of(width),
    )(maps, rows, *earlier)


def add_to(part, got):
    return (part.astype(F32) + got.astype(F32)).astype(BF)


def reduce_z(whole, z, second=(), third=(), last=()):
    parts = [lax.dynamic_index_in_dim(whole, (z + ahead) % NZ, 0, keepdims=False) for ahead in range(NZ)]
    half = whole.shape[2] // 256 * 128
    forth, back = shift(parts[4][:, :half], 1), shift(parts[4][:, half:], -1)
    forth = jnp.concatenate([add_to(parts[3][:, :half], forth), parts[3][:, half:]], axis=1)
    back = jnp.concatenate([parts[5][:, :half], add_to(parts[5][:, half:], back)], axis=1)
    if second:
        forth = after(forth, *second)
    forth = add_to(parts[2], shift(forth, 1))
    back = add_to(parts[6], shift(back, -1))
    if third:
        forth = after(forth, *third)
    forth = add_to(parts[1], shift(forth, 1))
    back = add_to(parts[7], shift(back, -1))
    if last:
        forth = after(forth, *last)
    forth, back = shift(forth, 1), shift(back, -1)
    return (parts[0].astype(F32) + forth.astype(F32) + back.astype(F32)).astype(BF)


def exchange_x(a):
    return lax.all_to_all(a, "x", split_axis=0, concat_axis=0, tiled=True)


def slot_map(ids, dropped, probs):
    experts = jnp.arange(EXPERTS, dtype=jnp.int32)
    named = ids.T[:, :, None] == experts[None, None, :]
    routed = jnp.any(named, axis=0)
    kept = jnp.any(named & (dropped.T == 0)[:, :, None], axis=0)
    order = jnp.arange(TOK, dtype=jnp.int32)
    earlier = (order[:, None] > order[None, :]).astype(BF)
    position = jnp.dot(earlier, routed.astype(BF), preferred_element_type=F32)
    slots = jnp.where(kept, position, -1.0)
    weights = jnp.sum(jnp.where(named, probs.T.astype(F32)[:, :, None], 0.0), axis=0)
    return slots.astype(BF), weights.astype(BF)


def spread(value, size):
    return jnp.full((size, 128), value, F32)


def all_values(values, axes):
    return lax.all_to_all(values, axes, split_axis=0, concat_axis=0, tiled=True)


def pass_kernel(*refs):
    pass


def after(value, *earlier):
    anywhere = pl.BlockSpec(memory_space=pl.ANY)
    return pl.pallas_call(
        pass_kernel,
        out_shape=jax.ShapeDtypeStruct(value.shape, value.dtype),
        in_specs=[anywhere] * (1 + len(earlier)),
        out_specs=anywhere,
        input_output_aliases={0: 0},
        compiler_params=pltpu.CompilerParams(vmem_limit_bytes=56 * 1024 * 1024),
        cost_estimate=pl.CostEstimate(flops=0, bytes_accessed=0, transcendentals=0),
    )(value, *earlier)


def body(tokens, out_grad, probs, expert_ids, dropped, preacts, w_gu, w_down):
    x, z = lax.axis_index("x"), lax.axis_index("z")
    slots, weights = slot_map(expert_ids, dropped, probs)
    w_down_full = lax.all_gather(w_down, ("y", "c"), axis=2, tiled=True)[0]
    w_gu_full = lax.all_gather(w_gu, ("y", "c"), axis=1, tiled=True)[0]
    info = jnp.concatenate([slots, weights, jnp.zeros((TOK, 64), BF)], axis=1)
    pre = preacts.reshape(NX * NZ * CAP, 2 * FW)
    flat = lambda a: a.reshape(NX * NZ * CAP, a.shape[2])

    blocks = gather_z(jnp.concatenate([out_grad[:, :WIDTH], info], axis=1))
    later_blocks = gather_z(out_grad[:, WIDTH:])
    first, maps = slots_first(z, blocks, w_down_full)
    tokens_all = lax.all_gather(tokens, "z", axis=0, tiled=True)
    first = exchange_x(first)
    second = exchange_x(after(slots_later(z, maps, later_blocks, w_gu_full), first))
    x_first = exchange_x(after(slots_whole(maps, tokens_all, 0, WIDTH), second))
    x_slots = slots_whole(maps, tokens_all, 1, WIDTH)

    dgu, hidden_p, tag = expert_pass(x * NZ + z, flat(first), flat(second), w_down_full, pre)
    grad_down = jnp.concatenate(
        [
            jnp.einsum("qf,qd->fd", hidden_p, p, preferred_element_type=F32)
            for p in (flat(first)[:, :WIDTH], flat(second))
        ],
        axis=1,
    ).astype(BF)
    sent = slot_grads(dgu, w_gu_full, tag, grad_down, 0, BACK, True)
    x_second = exchange_x(after(x_slots, x_first))
    sent_last = slot_grads(dgu, w_gu_full, tag, sent, BACK, D, False)
    back_first = exchange_x(after(sent, x_second, sent_last))
    grad_gu = jnp.concatenate(
        [jnp.einsum("qd,qf->df", flat(p), dgu, preferred_element_type=F32) for p in (x_first, x_second)], axis=0
    ).astype(BF)
    back_second = exchange_x(after(sent_last, back_first, grad_gu))

    scatter = lambda a, axis: lax.psum_scatter(a, ("y", "c"), scatter_dimension=axis, tiled=True).astype(F32)
    down_part = scatter(grad_down, 1)
    gu_part = scatter(grad_gu, 0)
    squares = spread(jnp.sum(gu_part * gu_part) + jnp.sum(down_part * down_part), NX * NZ)
    plane = all_values(squares, ("x", "z"))
    planes = all_values(spread(jnp.sum(plane[:, 0]), 8), ("y", "c"))
    mean_square = jnp.sum(planes[:, 0]) / (EXPERTS * 3 * D * FW)

    tok_first = reduce_z(combine(maps, back_first, grad_gu), z)
    tok_second = reduce_z(combine(maps, back_second, squares), z, (), (plane,), (planes,))
    tok_grad = jnp.concatenate([tok_first[:, :BACK], tok_second], axis=1)
    by_expert = tok_first[:, BACK : BACK + EXPERTS].astype(F32).T
    experts = jnp.arange(EXPERTS, dtype=jnp.int32)
    named = expert_ids.T[:, None, :] == experts[None, :, None]
    prob_grad = jnp.sum(jnp.where(named, by_expert[None], 0.0), axis=1)
    prob_grad = jnp.where(dropped.T == 0, prob_grad, 0.0).T.astype(BF)

    return tok_grad, prob_grad, gu_part[None], down_part[None], mean_square


def solution(mesh):
    split = Mesh(mesh.devices.reshape(4, 2, NX, NZ), ("y", "c", "x", "z"))
    rows = P(("y", "c", "x", "z"), None)
    gu, down = P(("x", "z"), ("y", "c"), None), P(("x", "z"), None, ("y", "c"))
    return jax.shard_map(
        body,
        mesh=split,
        in_specs=(rows, rows, rows, rows, rows, P(("y", "c"), ("x", "z"), None, None), gu, down),
        out_specs=(rows, rows, gu, down, P()),
        check_vma=False,
    )
```

```python
import jax
import jax.numpy as jnp
from jax import lax
from jax.experimental import pallas as pl
from jax.experimental.pallas import tpu as pltpu
from jax.sharding import Mesh, PartitionSpec as P

D = 2048
FW = 384
EXPERTS = 32
CAP = 40
TOK = 128
NX = 4
NZ = 8
CHUNKS = 2
WIDTH = D // CHUNKS
BF = jnp.bfloat16
F32 = jnp.float32


def shift(a, step):
    return lax.ppermute(a, "z", [(i, (i + step) % NZ) for i in range(NZ)])


def gather_z(block):
    half = block.shape[1] // 256 * 128
    forth, back = block, block
    blocks = [block] + [None] * 7
    for step in (1, 2, 3):
        forth, back = shift(forth, 1), shift(back, -1)
        blocks[NZ - step], blocks[step] = forth, back
    blocks[4] = shift(forth[:, :half], 1)
    blocks.append(shift(back[:, half:], -1))
    return blocks


def slot_rows(which, block, out_ref, pair, span):
    places = lax.broadcasted_iota(jnp.int32, (CAP, TOK), 0).astype(F32)
    halves = []
    for number in range(2):
        hits = [jnp.where(which(2 * pair + number, e) == places, 1.0, 0.0) for e in range(NX)]
        hits = jnp.concatenate(hits, axis=0).astype(BF)
        halves.append(jnp.dot(hits, block(2 * pair + number), preferred_element_type=F32))
    for e in range(NX):
        rows = [half[e * CAP : (e + 1) * CAP] for half in halves]
        out_ref[e, pl.ds(pair * 2 * CAP, 2 * CAP), span] = jnp.concatenate(rows, axis=0).astype(BF)


def spans(width):
    return [slice(at, min(at + 384, width)) for at in range(0, width, 384)]


def place_blocks(z, refs, held):
    width = held.shape[2]
    half = refs[4].shape[1]
    for ahead in range(NZ):
        at = lax.rem(z + ahead, NZ)
        if ahead == 4:
            held[at, :, :half] = refs[4][...]
            held[at, :, half:] = refs[8][...]
        else:
            held[at] = refs[ahead][...]


def first_kernel(z_ref, *refs):
    blocks, (out_ref, map_ref, held, flipped) = refs[:9], refs[9:]
    z = z_ref[0]
    place_blocks(z, blocks, held)
    for at in range(NZ):
        flipped[...] = held[at, :, WIDTH:].astype(F32).T
        for e in range(NX):
            map_ref[at, e : e + 1, :] = flipped[pl.ds(e * NZ + z, 1), :]
        map_ref[at, NX:, :] = jnp.zeros((8 - NX, TOK), F32)
    for span in spans(held.shape[2]):
        for pair in range(NZ // 2):
            slot_rows(lambda k, e: map_ref[k, e : e + 1, :], lambda k: held[k, :, span], out_ref, pair, span)


def later_kernel(z_ref, map_ref, *refs):
    blocks, (out_ref, held) = refs[:9], refs[9:]
    place_blocks(z_ref[0], blocks, held)
    for span in spans(held.shape[2]):
        for pair in range(NZ // 2):
            slot_rows(lambda k, e: map_ref[k, e : e + 1, :], lambda k: held[k, :, span], out_ref, pair, span)


VMEM = pl.BlockSpec(memory_space=pltpu.VMEM)
SMEM = pl.BlockSpec(memory_space=pltpu.SMEM)
PARAMS = pltpu.CompilerParams(vmem_limit_bytes=56 * 1024 * 1024)


def cost_of(width):
    return pl.CostEstimate(
        flops=2 * NZ * NX * CAP * TOK * width, bytes_accessed=2 * (NZ * TOK + NX * NZ * CAP) * width, transcendentals=0
    )


def slots_first(z, blocks):
    width = blocks[0].shape[1]
    return pl.pallas_call(
        first_kernel,
        out_shape=(
            jax.ShapeDtypeStruct((NX, NZ * CAP, width), BF),
            jax.ShapeDtypeStruct((NZ, 8, TOK), F32),
        ),
        in_specs=[SMEM] + [VMEM] * 9,
        out_specs=(VMEM, VMEM),
        scratch_shapes=[pltpu.VMEM((NZ, TOK, width), BF), pltpu.VMEM((128, TOK), F32)],
        compiler_params=PARAMS,
        cost_estimate=cost_of(width),
    )(z.reshape(1), *blocks)


def slots_later(z, maps, blocks):
    width = blocks[0].shape[1]
    return pl.pallas_call(
        later_kernel,
        out_shape=jax.ShapeDtypeStruct((NX, NZ * CAP, width), BF),
        in_specs=[SMEM] + [VMEM] * 10,
        out_specs=VMEM,
        scratch_shapes=[pltpu.VMEM((NZ, TOK, width), BF)],
        compiler_params=PARAMS,
        cost_estimate=cost_of(width),
    )(z.reshape(1), maps, *blocks)


def combine_kernel(map_ref, rows_ref, *refs):
    out_ref = refs[-1]
    places = lax.broadcasted_iota(jnp.int32, (CAP, TOK), 0).astype(F32)
    nothing = jnp.zeros((CAP, TOK), F32)
    width = rows_ref.shape[2]
    for pair in range(NZ // 2):
        hits = []
        for e in range(NX):
            here = [jnp.where(map_ref[2 * pair + n, e : e + 1, :] == places, 1.0, 0.0) for n in range(2)]
            hits.append(jnp.concatenate([here[0], nothing], axis=1))
            hits.append(jnp.concatenate([nothing, here[1]], axis=1))
        hits = jnp.concatenate(hits, axis=0).astype(BF)
        for span in spans(width):
            rows = [rows_ref[e, pair * 2 * CAP : (pair + 1) * 2 * CAP, span] for e in range(NX)]
            rows = jnp.concatenate(rows, axis=0)
            got = lax.dot_general(hits, rows, (((0,), (0,)), ((), ())), preferred_element_type=F32).astype(BF)
            out_ref[2 * pair, :, span] = got[:TOK]
            out_ref[2 * pair + 1, :, span] = got[TOK:]


def combine(maps, rows, *earlier):
    width = rows.shape[2]
    return pl.pallas_call(
        combine_kernel,
        out_shape=jax.ShapeDtypeStruct((NZ, TOK, width), BF),
        in_specs=[VMEM, VMEM] + [pl.BlockSpec(memory_space=pl.ANY)] * len(earlier),
        out_specs=VMEM,
        compiler_params=PARAMS,
        cost_estimate=cost_of(width),
    )(maps, rows, *earlier)


def add_to(part, got):
    return (part.astype(F32) + got.astype(F32)).astype(BF)


def reduce_z(whole, z):
    parts = [lax.dynamic_index_in_dim(whole, (z + ahead) % NZ, 0, keepdims=False) for ahead in range(NZ)]
    half = whole.shape[2] // 256 * 128
    forth, back = shift(parts[4][:, :half], 1), shift(parts[4][:, half:], -1)
    forth = jnp.concatenate([add_to(parts[3][:, :half], forth), parts[3][:, half:]], axis=1)
    back = jnp.concatenate([parts[5][:, :half], add_to(parts[5][:, half:], back)], axis=1)
    for ahead, behind in ((2, 6), (1, 7)):
        forth = add_to(parts[ahead], shift(forth, 1))
        back = add_to(parts[behind], shift(back, -1))
    forth, back = shift(forth, 1), shift(back, -1)
    return (parts[0].astype(F32) + forth.astype(F32) + back.astype(F32)).astype(BF)


def exchange_x(a):
    return lax.all_to_all(a, "x", split_axis=0, concat_axis=0, tiled=True)


def slot_map(ids, dropped, probs):
    experts = jnp.arange(EXPERTS, dtype=jnp.int32)
    named = ids.T[:, :, None] == experts[None, None, :]
    routed = jnp.any(named, axis=0)
    kept = jnp.any(named & (dropped.T == 0)[:, :, None], axis=0)
    order = jnp.arange(TOK, dtype=jnp.int32)
    earlier = (order[:, None] > order[None, :]).astype(BF)
    position = jnp.dot(earlier, routed.astype(BF), preferred_element_type=F32)
    slots = jnp.where(kept, position, -1.0)
    weights = jnp.sum(jnp.where(named, probs.T.astype(F32)[:, :, None], 0.0), axis=0)
    return slots.astype(BF), weights.astype(BF)


def spread(value, size):
    return jnp.full((size, 128), value, F32)


def all_values(values, axes):
    return lax.all_to_all(values, axes, split_axis=0, concat_axis=0, tiled=True)


def pass_kernel(*refs):
    pass


def touch(value, *earlier):
    anywhere = pl.BlockSpec(memory_space=pl.ANY)
    return pl.pallas_call(
        pass_kernel,
        out_shape=jax.ShapeDtypeStruct(value.shape, value.dtype),
        in_specs=[anywhere] * (1 + len(earlier)),
        out_specs=anywhere,
        input_output_aliases={0: 0},
        compiler_params=pltpu.CompilerParams(vmem_limit_bytes=56 * 1024 * 1024),
        cost_estimate=pl.CostEstimate(flops=0, bytes_accessed=0, transcendentals=0),
    )(value, *earlier)


def after(value, earlier):
    return lax.optimization_barrier((value, earlier))[0]


def body(tokens, out_grad, probs, expert_ids, dropped, preacts, w_gu, w_down):
    x, z = lax.axis_index("x"), lax.axis_index("z")
    slots, weights = slot_map(expert_ids, dropped, probs)
    w_down_full = lax.all_gather(w_down, ("y", "c"), axis=2, tiled=True)[0]
    w_gu_full = lax.all_gather(w_gu, ("y", "c"), axis=1, tiled=True)[0]
    lane = jnp.arange(128, dtype=jnp.int32)[None, :]
    info = jnp.concatenate([slots, weights, jnp.zeros((TOK, 64), BF)], axis=1)
    pre = preacts.reshape(NX * NZ * CAP, 2 * FW)
    cuts = [slice(i * WIDTH, (i + 1) * WIDTH) for i in range(CHUNKS)]
    slots_of = lambda a: exchange_x(a).reshape(NX * NZ * CAP, a.shape[2])

    blocks = gather_z(jnp.concatenate([out_grad[:, : WIDTH], info], axis=1))
    first, maps = slots_first(z, blocks)
    received = [slots_of(first)]
    for piece in (out_grad[:, WIDTH:], tokens[:, :WIDTH], tokens[:, WIDTH:]):
        blocks = gather_z(after(piece, blocks[2]))
        received.append(slots_of(slots_later(z, maps, blocks)))
    grad_in = [received[0][:, :WIDTH]] + received[1:CHUNKS]
    x_in = received[CHUNKS:]
    tag = received[0][:, WIDTH:].astype(F32)
    prob_in = jnp.sum(jnp.where(lane == EXPERTS + x * NZ + z, tag, 0.0), axis=1)

    proj = 0.0
    for cut, piece in zip(cuts, grad_in):
        proj = proj + jnp.einsum("qd,fd->qf", piece, w_down_full[:, cut], preferred_element_type=F32)
    gate_pre = pre[:, :FW].astype(F32)
    up_pre = pre[:, FW:].astype(F32)
    sigmoid_a = jax.nn.sigmoid(gate_pre)
    silu_a = gate_pre * sigmoid_a
    hidden = silu_a * up_pre
    slot_prob = jnp.sum(hidden * proj, axis=-1).astype(BF)
    scaled = prob_in[:, None] * proj
    dgu = jnp.concatenate(
        [scaled * up_pre * sigmoid_a * (1.0 + gate_pre * (1.0 - sigmoid_a)), scaled * silu_a], axis=-1
    ).astype(BF)
    hidden_p = (prob_in[:, None] * hidden).astype(BF)

    grad_down = jnp.concatenate(
        [jnp.einsum("qf,qd->fd", hidden_p, p, preferred_element_type=F32) for p in grad_in], axis=1
    ).astype(BF)
    grad_gu = jnp.concatenate(
        [jnp.einsum("qd,qf->df", p, dgu, preferred_element_type=F32) for p in x_in], axis=0
    ).astype(BF)
    settled = [grad_down, grad_gu]
    grad_down = lax.psum_scatter(grad_down[None], ("y", "c"), scatter_dimension=2, tiled=True).astype(F32)
    grad_gu = lax.psum_scatter(grad_gu[None], ("y", "c"), scatter_dimension=1, tiled=True).astype(F32)

    returned = []
    for number, cut in enumerate(cuts):
        slot_grad = jnp.einsum("qf,df->qd", dgu, w_gu_full[cut], preferred_element_type=F32).astype(BF)
        if number == 0:
            tag = jnp.where(lane == x * NZ + z, slot_prob[:, None], jnp.zeros((), BF))
            slot_grad = jnp.concatenate([slot_grad, tag], axis=1)
        width = slot_grad.shape[1]
        back = exchange_x(touch(slot_grad.reshape(NX, NZ * CAP, width), settled[number]))
        parts = combine(maps, back)
        returned.append(reduce_z(parts, z))
    tok_grad = jnp.concatenate([returned[0][:, :WIDTH]] + returned[1:], axis=1)
    by_expert = returned[0][:, WIDTH : WIDTH + EXPERTS].astype(F32).T
    experts = jnp.arange(EXPERTS, dtype=jnp.int32)
    named = expert_ids.T[:, None, :] == experts[None, :, None]
    prob_grad = jnp.sum(jnp.where(named, by_expert[None], 0.0), axis=1)
    prob_grad = jnp.where(dropped.T == 0, prob_grad, 0.0).T.astype(BF)

    partial_sq = jnp.sum(grad_gu * grad_gu) + jnp.sum(grad_down * grad_down)
    plane = all_values(spread(partial_sq, NX * NZ), ("x", "z"))
    planes = all_values(spread(jnp.sum(plane[:, 0]), 8), ("y", "c"))
    mean_square = jnp.sum(planes[:, 0]) / (EXPERTS * 3 * D * FW)
    return tok_grad, prob_grad, grad_gu, grad_down, mean_square


def solution(mesh):
    split = Mesh(mesh.devices.reshape(4, 2, NX, NZ), ("y", "c", "x", "z"))
    rows = P(("y", "c", "x", "z"), None)
    gu, down = P(("x", "z"), ("y", "c"), None), P(("x", "z"), None, ("y", "c"))
    return jax.shard_map(
        body,
        mesh=split,
        in_specs=(rows, rows, rows, rows, rows, P(("y", "c"), ("x", "z"), None, None), gu, down),
        out_specs=(rows, rows, gu, down, P()),
        check_vma=False,
    )
```

```python
import jax
import jax.numpy as jnp
from jax import lax
from jax.experimental import pallas as pl
from jax.sharding import Mesh, PartitionSpec as P

D = 2048
FW = 384
EXPERTS = 32
CAP = 40
TOK = 128
NX = 4
NZ = 8
CHUNKS = 2
WIDTH = D // CHUNKS
BF = jnp.bfloat16
F32 = jnp.float32


def shift(a, step):
    return lax.ppermute(a, "z", [(i, (i + step) % NZ) for i in range(NZ)])


def gather_z(block):
    half = block.shape[1] // 256 * 128
    forth, back = block, block
    blocks = [block] + [None] * 7
    for step in (1, 2, 3):
        forth, back = shift(forth, 1), shift(back, -1)
        blocks[NZ - step], blocks[step] = forth, back
    blocks[4] = jnp.concatenate([shift(forth[:, :half], 1), shift(back[:, half:], -1)], axis=1)
    return jnp.stack(blocks), blocks[2]


def add_to(part, got):
    return (part.astype(F32) + got.astype(F32)).astype(BF)


def reduce_z(parts):
    half = parts.shape[2] // 256 * 128
    forth, back = shift(parts[4][:, :half], 1), shift(parts[4][:, half:], -1)
    forth = jnp.concatenate([add_to(parts[3][:, :half], forth), parts[3][:, half:]], axis=1)
    back = jnp.concatenate([parts[5][:, :half], add_to(parts[5][:, half:], back)], axis=1)
    for ahead, behind in ((2, 6), (1, 7)):
        forth = add_to(parts[ahead], shift(forth, 1))
        back = add_to(parts[behind], shift(back, -1))
    forth, back = shift(forth, 1), shift(back, -1)
    return (parts[0].astype(F32) + forth.astype(F32) + back.astype(F32)).astype(BF)


def exchange_x(a):
    return lax.all_to_all(a, "x", split_axis=0, concat_axis=0, tiled=True)


def turned(a, axis, start):
    return lax.dynamic_slice_in_dim(jnp.concatenate([a, a], axis=axis), start, NZ, axis)


def slot_map(ids, dropped, probs):
    experts = jnp.arange(EXPERTS, dtype=jnp.int32)
    named = ids.T[:, :, None] == experts[None, None, :]
    routed = jnp.any(named, axis=0)
    kept = jnp.any(named & (dropped.T == 0)[:, :, None], axis=0)
    order = jnp.arange(TOK, dtype=jnp.int32)
    earlier = (order[:, None] > order[None, :]).astype(BF)
    position = jnp.dot(earlier, routed.astype(BF), preferred_element_type=F32)
    slots = jnp.where(kept, position, -1.0)
    weights = jnp.sum(jnp.where(named, probs.T.astype(F32)[:, :, None], 0.0), axis=0)
    return slots.astype(BF), weights.astype(BF)


def spread(value, size):
    return jnp.full((size, 128), value, F32)


def all_values(values, axes):
    return lax.all_to_all(values, axes, split_axis=0, concat_axis=0, tiled=True)


def pass_kernel(*refs):
    pass


def touch(value, *earlier):
    anywhere = pl.BlockSpec(memory_space=pl.ANY)
    return pl.pallas_call(
        pass_kernel,
        out_shape=jax.ShapeDtypeStruct(value.shape, value.dtype),
        in_specs=[anywhere] * (1 + len(earlier)),
        out_specs=anywhere,
        input_output_aliases={0: 0},
        cost_estimate=pl.CostEstimate(flops=0, bytes_accessed=0, transcendentals=0),
    )(value, *earlier)


def after(value, earlier):
    return lax.optimization_barrier((value, earlier))[0]


def body(tokens, out_grad, probs, expert_ids, dropped, preacts, w_gu, w_down):
    x, z = lax.axis_index("x"), lax.axis_index("z")
    slots, weights = slot_map(expert_ids, dropped, probs)
    w_down_full = lax.all_gather(w_down, ("y", "c"), axis=2, tiled=True)[0]
    w_gu_full = lax.all_gather(w_gu, ("y", "c"), axis=1, tiled=True)[0]
    places = jnp.arange(CAP, dtype=jnp.int32).astype(F32)
    lane = jnp.arange(128, dtype=jnp.int32)[None, :]
    info = jnp.concatenate([slots, weights, jnp.zeros((TOK, 64), BF)], axis=1)
    pre = turned(preacts.reshape(NX, NZ, CAP, 2 * FW), 1, z).reshape(NX * NZ * CAP, 2 * FW)
    cuts = [slice(i * WIDTH, (i + 1) * WIDTH) for i in range(CHUNKS)]

    pieces = [out_grad[:, cut] for cut in cuts] + [tokens[:, cut] for cut in cuts]
    pieces[0] = jnp.concatenate([pieces[0], info], axis=1)
    gathered, mark = [], None
    for piece in pieces:
        blocks, mark = gather_z(piece if mark is None else after(piece, mark))
        gathered.append(blocks)
    maps = gathered[0][:, :, WIDTH : WIDTH + EXPERTS].reshape(NZ, TOK, NX, NZ)
    maps = lax.dynamic_index_in_dim(maps, z, 3, keepdims=False).transpose(0, 2, 1).astype(F32)
    onehot = (maps[:, :, None, :] == places[None, None, :, None]).astype(BF)
    onehot = onehot.reshape(NZ, NX * CAP, TOK)

    def to_slots(blocks):
        width = blocks.shape[2]
        rows = jnp.einsum("ost,otd->osd", onehot, blocks, preferred_element_type=F32).astype(BF)
        rows = rows.reshape(NZ, NX, CAP, width).transpose(1, 0, 2, 3)
        return exchange_x(rows.reshape(NX, NZ * CAP, width)).reshape(NX * NZ * CAP, width)

    received = [to_slots(blocks) for blocks in gathered]
    grad_in = [received[0][:, :WIDTH]] + received[1:CHUNKS]
    x_in = received[CHUNKS:]
    tag = received[0][:, WIDTH:].astype(F32)
    prob_in = jnp.sum(jnp.where(lane == EXPERTS + x * NZ + z, tag, 0.0), axis=1)

    proj = 0.0
    for cut, piece in zip(cuts, grad_in):
        proj = proj + jnp.einsum("qd,fd->qf", piece, w_down_full[:, cut], preferred_element_type=F32)
    gate_pre = pre[:, :FW].astype(F32)
    up_pre = pre[:, FW:].astype(F32)
    sigmoid_a = jax.nn.sigmoid(gate_pre)
    silu_a = gate_pre * sigmoid_a
    hidden = silu_a * up_pre
    slot_prob = jnp.sum(hidden * proj, axis=-1).astype(BF)
    scaled = prob_in[:, None] * proj
    dgu = jnp.concatenate(
        [scaled * up_pre * sigmoid_a * (1.0 + gate_pre * (1.0 - sigmoid_a)), scaled * silu_a], axis=-1
    ).astype(BF)
    hidden_p = (prob_in[:, None] * hidden).astype(BF)

    grad_down = jnp.concatenate(
        [jnp.einsum("qf,qd->fd", hidden_p, p, preferred_element_type=F32) for p in grad_in], axis=1
    ).astype(BF)
    grad_gu = jnp.concatenate(
        [jnp.einsum("qd,qf->df", p, dgu, preferred_element_type=F32) for p in x_in], axis=0
    ).astype(BF)
    settled = [grad_down, grad_gu]

    returned = []
    for number, cut in enumerate(cuts):
        slot_grad = jnp.einsum("qf,df->qd", dgu, w_gu_full[cut], preferred_element_type=F32).astype(BF)
        if number == 0:
            tag = jnp.where(lane == x * NZ + z, slot_prob[:, None], jnp.zeros((), BF))
            slot_grad = jnp.concatenate([slot_grad, tag], axis=1)
        width = slot_grad.shape[1]
        back = exchange_x(touch(slot_grad.reshape(NX, NZ * CAP, width), settled[number]))
        back = back.reshape(NX, NZ, CAP, width).transpose(1, 0, 2, 3).reshape(NZ, NX * CAP, width)
        parts = jnp.einsum("ost,osd->otd", onehot, back, preferred_element_type=F32).astype(BF)
        returned.append(reduce_z(parts))
    tok_grad = jnp.concatenate([returned[0][:, :WIDTH]] + returned[1:], axis=1)
    by_expert = returned[0][:, WIDTH : WIDTH + EXPERTS].astype(F32).T
    experts = jnp.arange(EXPERTS, dtype=jnp.int32)
    named = expert_ids.T[:, None, :] == experts[None, :, None]
    prob_grad = jnp.sum(jnp.where(named, by_expert[None], 0.0), axis=1)
    prob_grad = jnp.where(dropped.T == 0, prob_grad, 0.0).T.astype(BF)

    grad_down = lax.psum_scatter(grad_down[None], ("y", "c"), scatter_dimension=2, tiled=True).astype(F32)
    grad_gu = lax.psum_scatter(grad_gu[None], ("y", "c"), scatter_dimension=1, tiled=True).astype(F32)
    partial_sq = jnp.sum(grad_gu * grad_gu) + jnp.sum(grad_down * grad_down)
    plane = all_values(spread(partial_sq, NX * NZ), ("x", "z"))
    planes = all_values(spread(jnp.sum(plane[:, 0]), 8), ("y", "c"))
    mean_square = jnp.sum(planes[:, 0]) / (EXPERTS * 3 * D * FW)
    return tok_grad, prob_grad, grad_gu, grad_down, mean_square


def solution(mesh):
    split = Mesh(mesh.devices.reshape(4, 2, NX, NZ), ("y", "c", "x", "z"))
    rows = P(("y", "c", "x", "z"), None)
    gu, down = P(("x", "z"), ("y", "c"), None), P(("x", "z"), None, ("y", "c"))
    return jax.shard_map(
        body,
        mesh=split,
        in_specs=(rows, rows, rows, rows, rows, P(("y", "c"), ("x", "z"), None, None), gu, down),
        out_specs=(rows, rows, gu, down, P()),
        check_vma=False,
    )
```
